32 devices in a mesh: groups: 2 (over y), prob: 16 (over z, x, core).
Axes of the slice: x: 2, y: 2, z: 4, core: 2. Of those that a mesh axis runs over, the one named last changes fastest.
Arguments:
- segment_queries: bfloat16 [32, 4, 64, 8192], P(('groups', 'prob')), parts along dimension 0, may hold values from -18 to 18
- segment_kv: bfloat16 [32, 4, 2, 64, 1024], P(('groups', 'prob')), parts along dimension 0, may hold values from -18 to 18
- prefix_kv: bfloat16 [32, 2, 256, 1024], P(('groups', 'prob')), parts along dimension 0, may hold values from -6 to 6
- page_pool: bfloat16 [2048, 2, 8, 1024], P(('groups', 'prob')), parts along dimension 0, may hold values from -6 to 6
- beam_count: int32 [32], P(('groups', 'prob')), parts along dimension 0, may hold values from 1 to 4, as said below
- page_version: int32 [32, 4, 16], P(('groups', 'prob')), parts along dimension 0, may hold values from 0 to 3, as said below
- page_slot: int32 [32, 16, 4], P(('groups', 'prob')), parts along dimension 0, may hold values from 0 to 63, as said below
Outputs:
- attention_out: bfloat16 [32, 4, 64, 8192], P(('groups', 'prob')), parts along dimension 0
The draws below stay inside these ranges and needn't reach their ends.
There are 2 independent parts, one for each index of `groups`. The reference program is written for one: setup_inputs(seed, part) draws one part's arguments, and reference() takes and returns one part's arrays. A program takes and returns all parts, laid end to end along the dimension named above; each array names one. Nothing has to cross between parts.
Inputs may be any that keep to these rules, and one draw needn't show every extreme that they name: `beam_count`: live beams of each problem; some problem has 4 in every draw. `page_version`: beam 0 reads version 0 of every page; every other beam b reads the versions of an earlier beam of its problem up to some page and version b from there on, its last page always version b. Version v of context page j of problem p is page_pool row d * 64 + page_slot[p, j, v] with d = (p + 1 + j * 4 + v) mod 16; every pool row is named by exactly one (p, j, v).
All inputs are finite; a program needn't handle non-finite values.
Results may differ from the reference program's by a relative error of at most 0.007.
Values may be sent and summed in bfloat16 or wider, within the bound.
A program may use at most 128 MiB of HBM per device.

```python
import math
import jax
import jax.numpy as jnp
from jax import lax

QH = 64
KVH = 8
HD = 128
KVW = 1024
BEAMS = 4
SEG = 64
SHARED = 256
CTX_PAGES = 16
PAGE = 8
PROBS = 16
KMAX = 64


def draw_segment_queries(key, part):
    key = jax.random.fold_in(key, 21)
    shape = (PROBS, BEAMS, SEG, KVH, QH // KVH, HD)
    base = jax.random.truncated_normal(key, -4.0, 4.0, shape, jnp.float32)
    return base.reshape(PROBS, BEAMS, SEG, QH * HD).astype(jnp.bfloat16)


def draw_segment_kv(key, part):
    key = jax.random.fold_in(key, 22)
    shape = (PROBS, BEAMS, 2, SEG, KVH, HD)
    base = jax.random.truncated_normal(key, -4.0, 4.0, shape, jnp.float32)
    return base.reshape(PROBS, BEAMS, 2, SEG, KVH * HD).astype(jnp.bfloat16)


def draw_beam_count(key, part):
    key = jax.random.fold_in(key, 11)
    pick_key, forced_key = jax.random.split(key)
    picked = jax.random.randint(pick_key, (PROBS,), 0, 20)
    counts = 1 + (picked >= 8).astype(jnp.int32) + (picked >= 14).astype(jnp.int32) + (picked >= 17).astype(jnp.int32)
    counts = jnp.clip(counts, 1, BEAMS)
    forced = jax.random.randint(forced_key, (), 0, PROBS)
    return jnp.where(jnp.arange(PROBS) == forced, BEAMS, counts).astype(jnp.int32)


def draw_page_version(key, part):
    key = jax.random.fold_in(key, 12)
    page_numbers = jnp.arange(CTX_PAGES, dtype=jnp.int32)[None, :]
    rows = [jnp.zeros((PROBS, CTX_PAGES), jnp.int32)]
    for beam_number in range(1, BEAMS):
        parent_key, split_key = jax.random.split(jax.random.fold_in(key, beam_number))
        parents = jax.random.randint(parent_key, (PROBS,), 0, beam_number)
        divergence = jax.random.randint(split_key, (PROBS,), 0, CTX_PAGES)
        earlier = jnp.stack(rows, axis=1)
        parent_row = earlier[jnp.arange(PROBS), parents]
        rows.append(jnp.where(page_numbers < divergence[:, None], parent_row, beam_number).astype(jnp.int32))
    return jnp.stack(rows, axis=1).astype(jnp.int32)


def draw_page_slot(key, part):
    key = jax.random.fold_in(key, 13)
    orders = jax.vmap(lambda device: jax.random.permutation(jax.random.fold_in(key, device), KMAX))(jnp.arange(PROBS))
    copies = jnp.arange(CTX_PAGES, dtype=jnp.int32)[:, None] * BEAMS + jnp.arange(BEAMS, dtype=jnp.int32)[None, :]
    owners = (jnp.arange(PROBS, dtype=jnp.int32)[:, None, None] + 1 + copies[None]) % PROBS
    return orders[owners, jnp.broadcast_to(copies[None], owners.shape)].astype(jnp.int32)


def shard_levels(rng, shape, pieces, least, largest):
    def one(position, shards_of):
        heights = jax.random.uniform(jax.random.fold_in(jax.random.fold_in(rng, 6), position), (shards_of,), jnp.float32, least / len(pieces), largest / len(pieces))
        return jnp.repeat(jnp.exp(heights), shape[position] // shards_of).reshape((-1,) + (1,) * (len(shape) - position - 1))

    loudness = one(*pieces[0])
    for cut in pieces[1:]:
        loudness = loudness * one(*cut)
    return loudness


def scatter_about(stream_key, dims, scale, most, cuts=(), kind=jnp.bfloat16):
    array = scale * jax.random.normal(stream_key, dims, jnp.float32)
    if cuts:
        array = array * shard_levels(stream_key, dims, cuts, -0.22, 0.18)
    return jnp.clip(array, -most, most).astype(kind)


def setup_inputs(seed: int = 0, part: int = 0) -> dict:
    splits = jax.random.split(jax.random.key(seed), 8)
    own_keys = jax.random.split(jax.random.fold_in(splits[7], part), 8)
    return {
        "segment_queries": draw_segment_queries(jax.random.fold_in(jax.random.fold_in(splits[7], part), 71), part),
        "segment_kv": draw_segment_kv(jax.random.fold_in(jax.random.fold_in(splits[7], part), 71), part),
        "prefix_kv": scatter_about(own_keys[2], (PROBS, 2, SHARED, KVW), 1.0, 6.0, ((0, 16),)),
        "page_pool": scatter_about(own_keys[3], (PROBS * KMAX, 2, PAGE, KVW), 1.0, 6.0, ((0, 16),)),
        "beam_count": draw_beam_count(jax.random.fold_in(jax.random.fold_in(splits[7], part), 71), part),
        "page_version": draw_page_version(jax.random.fold_in(jax.random.fold_in(splits[7], part), 71), part),
        "page_slot": draw_page_slot(jax.random.fold_in(jax.random.fold_in(splits[7], part), 71), part),
    }


NEG_FILL = -1e+30

def rotary_table(length, offset, width):
    half_width = width // 2
    frequency = jnp.exp(jnp.arange(half_width, dtype=jnp.float32) * (-2.0 * math.log(1000000.0) / width))
    positions = jnp.arange(length, dtype=jnp.float32) + offset
    angles = positions[:, None] * frequency[None, :]
    return (jnp.cos(angles), jnp.sin(angles))

def rotary(values, cosine, sine_table):
    floats = values.astype(jnp.float32)
    half_width = floats.shape[-1] // 2
    first_half = floats[..., :half_width]
    second_half = floats[..., half_width:]
    cos_rows = cosine[:, None, :]
    sin_rows = sine_table[:, None, :]
    turned = jnp.concatenate([first_half * cos_rows - second_half * sin_rows, second_half * cos_rows + first_half * sin_rows], axis=-1)
    return turned.astype(jnp.bfloat16)

def attend(queries, prefix, paged_kv, fresh_kv):
    seg_len = queries.shape[0]
    grouped = queries.reshape(seg_len, KVH, QH // KVH, HD).astype(jnp.float32)
    score_scale = 1.0 / math.sqrt(HD)
    causal = jnp.arange(seg_len)[:, None] >= jnp.arange(seg_len)[None, :]

    def key_scores(source):
        key_rows = source[0].reshape(source.shape[1], KVH, HD).astype(jnp.float32)
        return jnp.einsum('tkgd,lkd->kgtl', grouped, key_rows) * score_scale

    def value_mix(weights, source):
        value_rows = source[1].reshape(source.shape[1], KVH, HD).astype(jnp.float32)
        return jnp.einsum('kgtl,lkd->tkgd', weights.astype(jnp.float32), value_rows)
    prefix_scores = key_scores(prefix)
    paged_scores = key_scores(paged_kv)
    fresh_scores = jnp.where(causal, key_scores(fresh_kv), NEG_FILL)
    row_max = jnp.maximum(jnp.maximum(prefix_scores.max(-1, keepdims=True), paged_scores.max(-1, keepdims=True)), fresh_scores.max(-1, keepdims=True))
    prefix_exp = jnp.exp(prefix_scores - row_max)
    paged_exp = jnp.exp(paged_scores - row_max)
    fresh_exp = jnp.where(causal, jnp.exp(fresh_scores - row_max), 0.0)
    totals = prefix_exp.sum(-1, keepdims=True) + paged_exp.sum(-1, keepdims=True) + fresh_exp.sum(-1, keepdims=True)
    mixed = value_mix((prefix_exp / totals).astype(jnp.bfloat16), prefix)
    mixed = mixed + value_mix((paged_exp / totals).astype(jnp.bfloat16), paged_kv)
    mixed = mixed + value_mix((fresh_exp / totals).astype(jnp.bfloat16), fresh_kv)
    return mixed.reshape(seg_len, QH * HD).astype(jnp.bfloat16)

def reference(segment_queries, segment_kv, prefix_kv, page_pool, beam_count, page_version, page_slot):
    pool = page_pool.reshape(PROBS, KMAX, 2, PAGE, KVW)
    cosine, sine_table = rotary_table(SEG, SHARED + CTX_PAGES * PAGE, HD)
    page_numbers = jnp.arange(CTX_PAGES, dtype=jnp.int32)

    def per_problem(problem):

        def per_beam(beam_number):
            versions = page_version[problem, beam_number].astype(jnp.int32)
            owners = (problem + 1 + page_numbers * BEAMS + versions) % PROBS
            fetched = pool[owners, page_slot[problem, page_numbers, versions]]
            paged_kv = jnp.transpose(fetched, (1, 0, 2, 3)).reshape(2, CTX_PAGES * PAGE, KVW)
            queries = rotary(segment_queries[problem, beam_number].reshape(SEG, QH, HD), cosine, sine_table).reshape(SEG, QH * HD)
            fresh_keys = rotary(segment_kv[problem, beam_number, 0].reshape(SEG, KVH, HD), cosine, sine_table).reshape(SEG, KVW)
            fresh_kv = jnp.stack([fresh_keys, segment_kv[problem, beam_number, 1]])
            result = attend(queries, prefix_kv[problem], paged_kv, fresh_kv)
            return jnp.where(beam_number < beam_count[problem], result, jnp.zeros_like(result))
        return lax.map(per_beam, jnp.arange(BEAMS, dtype=jnp.int32))
    return lax.map(per_problem, jnp.arange(PROBS, dtype=jnp.int32))
```

```python
import functools
import math

import jax
import jax.numpy as jnp
import numpy as np
from jax import lax
from jax.experimental import pallas as pl
from jax.experimental.pallas import tpu as pltpu
from jax.sharding import PartitionSpec as P

HD = 128
NEG_FILL = -1e30
LOG2_SCALE = math.log2(math.e) / math.sqrt(HD)


def rotary_tables(length, offset):
    half = HD // 2
    frequency = np.exp(np.arange(half) * (-2.0 * math.log(1000000.0) / HD))
    angles = (np.arange(length) + offset)[:, None] * frequency[None, :]
    cosine, sine = np.cos(angles), np.sin(angles)
    return (
        jnp.asarray(np.concatenate([cosine, cosine], axis=1), jnp.float32),
        jnp.asarray(np.concatenate([-sine, sine], axis=1), jnp.float32),
    )


def rotate(values, cosine, signed_sine):
    floats = values.astype(jnp.float32)
    swapped = pltpu.roll(floats, HD // 2, 1)
    return (floats * cosine + swapped * signed_sine).astype(jnp.bfloat16)


def dot_keys(queries, keys):
    return lax.dot_general(
        queries, keys, (((1,), (1,)), ((), ())), preferred_element_type=jnp.float32
    )


def dot_values(weights, values):
    extended = jnp.concatenate([values, jnp.ones_like(values)], axis=1)
    return jnp.dot(weights, extended, preferred_element_type=jnp.float32)


def local_part(q_ref, seg_ref, prefix_ref, cos_ref, sin_ref, rot_ref, acc_ref, ml_ref):
    seg_len = q_ref.shape[2]
    kv_heads = rot_ref.shape[1]
    group = q_ref.shape[3] // HD // kv_heads
    rows = group * seg_len
    cosine, sine = cos_ref[...], sin_ref[...]
    token = lax.broadcasted_iota(jnp.int32, (group, seg_len, seg_len), 1).reshape(rows, seg_len)
    key = lax.broadcasted_iota(jnp.int32, (rows, seg_len), 1)
    causal = token >= key
    lane = lax.broadcasted_iota(jnp.int32, (rows, HD), 1)
    for head in range(kv_heads):
        queries = jnp.concatenate(
            [
                rotate(q_ref[0, 0, :, pl.ds((head * group + g) * HD, HD)], cosine, sine)
                for g in range(group)
            ],
            axis=0,
        )
        columns = pl.ds(head * HD, HD)
        fresh_keys = rotate(seg_ref[0, 0, 0, :, columns], cosine, sine)
        prefix_scores = dot_keys(queries, prefix_ref[0, 0, :, columns])
        fresh_scores = jnp.where(causal, dot_keys(queries, fresh_keys), NEG_FILL)
        row_max = jnp.maximum(
            prefix_scores.max(-1, keepdims=True), fresh_scores.max(-1, keepdims=True)
        )
        shift = row_max * LOG2_SCALE
        prefix_exp = jnp.exp2(prefix_scores * LOG2_SCALE - shift).astype(jnp.bfloat16)
        fresh_exp = jnp.exp2(fresh_scores * LOG2_SCALE - shift).astype(jnp.bfloat16)
        mixed = dot_values(prefix_exp, prefix_ref[0, 1, :, columns]) + dot_values(
            fresh_exp, seg_ref[0, 0, 1, :, columns]
        )
        rot_ref[0, head] = queries
        acc_ref[0, head] = mixed[:, :HD]
        ml_ref[0, head] = jnp.where(lane < HD // 2, shift, mixed[:, HD:])


def paged_part(
    index_ref, count_ref, rot_ref, acc_ref, ml_ref, pages_ref, out_ref
):
    beam = pl.program_id(0)
    kv_heads = rot_ref.shape[1]
    seg_len = out_ref.shape[2]
    group = out_ref.shape[3] // HD // kv_heads
    pages = index_ref.shape[1]
    live = beam < count_ref[0]
    for head in range(kv_heads):
        columns = pl.ds(head * HD, HD)

        def gathered(which):
            return jnp.concatenate(
                [
                    pages_ref[index_ref[beam, j], which, :, columns].astype(jnp.float32)
                    for j in range(pages)
                ],
                axis=0,
            ).astype(jnp.bfloat16)

        scores = dot_keys(rot_ref[0, head], gathered(0)) * LOG2_SCALE
        packed = ml_ref[0, head]
        old_shift, old_total = packed[:, :1], packed[:, HD - 1 :]
        shift = jnp.maximum(old_shift, scores.max(-1, keepdims=True))
        weights = jnp.exp2(scores - shift).astype(jnp.bfloat16)
        decay = jnp.exp2(old_shift - shift)
        mixed = dot_values(weights, gathered(1))
        total = mixed[:, HD:] + old_total * decay
        result = (mixed[:, :HD] + acc_ref[0, head] * decay) / total
        result = jnp.where(live, result, 0.0).astype(jnp.bfloat16)
        for g in range(group):
            out_ref[0, 0, :, pl.ds((head * group + g) * HD, HD)] = result[
                g * seg_len : (g + 1) * seg_len
            ]


def per_device(
    segment_queries, segment_kv, prefix_kv, page_pool, beam_count, page_version, page_slot
):
    devices = lax.axis_size("prob")
    myself = lax.axis_index("prob")
    _, beams, seg_len, model_width = segment_queries.shape
    shared = prefix_kv.shape[2]
    pool_pages, _, page_len, kv_width = page_pool.shape
    context_pages = page_version.shape[2]
    kv_heads = kv_width // HD
    rows = model_width // kv_width * seg_len
    capacity = (pool_pages + devices - 1) // devices
    cosine, sine = rotary_tables(seg_len, shared + context_pages * page_len)

    slots = page_slot.reshape(-1)
    slots = jnp.pad(slots, (0, capacity * devices - slots.shape[0]))
    wanted = slots.reshape(capacity, devices).T
    requests = wanted[(jnp.arange(devices) - myself - 1) % devices]
    asked = lax.all_to_all(requests, "prob", split_axis=0, concat_axis=0, tiled=True)
    located = page_pool[asked.reshape(-1)].reshape(devices, capacity, 2, page_len, kv_width)
    received = lax.all_to_all(located, "prob", split_axis=0, concat_axis=0, tiled=True)
    received = received.reshape(devices * capacity, 2, page_len, kv_width)
    copy_index = jnp.arange(context_pages, dtype=jnp.int32)[None, :] * beams + page_version[0]
    index = (myself + 1 + copy_index) % devices * capacity + copy_index // devices

    per_head = lambda b: (b, 0, 0, 0)
    head_block = pl.BlockSpec((1, kv_heads, rows, HD), per_head)
    params = pltpu.CompilerParams(vmem_limit_bytes=48 * 1024 * 1024)
    flops = 4 * beams * kv_heads * rows * HD
    rot, acc, ml = pl.pallas_call(
        local_part,
        grid=(beams,),
        in_specs=[
            pl.BlockSpec((1, 1, seg_len, model_width), lambda b: (0, b, 0, 0)),
            pl.BlockSpec((1, 1, 2, seg_len, kv_width), lambda b: (0, b, 0, 0, 0)),
            pl.BlockSpec((1, 2, shared, kv_width), lambda b: (0, 0, 0, 0)),
            pl.BlockSpec((seg_len, HD), lambda b: (0, 0)),
            pl.BlockSpec((seg_len, HD), lambda b: (0, 0)),
        ],
        out_specs=[head_block, head_block, head_block],
        out_shape=[
            jax.ShapeDtypeStruct((beams, kv_heads, rows, HD), jnp.bfloat16),
            jax.ShapeDtypeStruct((beams, kv_heads, rows, HD), jnp.float32),
            jax.ShapeDtypeStruct((beams, kv_heads, rows, HD), jnp.float32),
        ],
        compiler_params=params,
        cost_estimate=pl.CostEstimate(
            flops=flops * (shared + seg_len),
            bytes_accessed=30 * 1024 * 1024,
            transcendentals=beams * kv_heads * rows * (shared + seg_len),
        ),
        name="local_part",
    )(segment_queries, segment_kv, prefix_kv, cosine, sine)
    grid_spec = pltpu.PrefetchScalarGridSpec(
        num_scalar_prefetch=2,
        grid=(beams,),
        in_specs=[
            pl.BlockSpec((1, kv_heads, rows, HD), lambda b, *_: (b, 0, 0, 0)),
            pl.BlockSpec((1, kv_heads, rows, HD), lambda b, *_: (b, 0, 0, 0)),
            pl.BlockSpec((1, kv_heads, rows, HD), lambda b, *_: (b, 0, 0, 0)),
            pl.BlockSpec(received.shape, lambda b, *_: (0, 0, 0, 0)),
        ],
        out_specs=pl.BlockSpec((1, 1, seg_len, model_width), lambda b, *_: (0, b, 0, 0)),
    )
    return pl.pallas_call(
        paged_part,
        grid_spec=grid_spec,
        out_shape=jax.ShapeDtypeStruct(segment_queries.shape, jnp.bfloat16),
        compiler_params=params,
        name="paged_part",
    )(index, beam_count, rot, acc, ml, received)


def solution(mesh):
    placed = (
        P(("groups", "prob"), None, None, None),
        P(("groups", "prob"), None, None, None, None),
        P(("groups", "prob"), None, None, None),
        P(("groups", "prob"), None, None, None),
        P(("groups", "prob")),
        P(("groups", "prob"), None, None),
        P(("groups", "prob"), None, None),
    )
    return jax.shard_map(
        per_device,
        mesh=mesh,
        in_specs=placed,
        out_specs=P(("groups", "prob"), None, None, None),
        check_vma=False,
    )
```

```python
import functools
import math

import jax
import jax.numpy as jnp
import numpy as np
from jax import lax
from jax.experimental import pallas as pl
from jax.experimental.pallas import tpu as pltpu
from jax.sharding import PartitionSpec as P

HD = 128
NEG_FILL = -1e30
MESH = pl.DeviceIdType.MESH
UNROLL = 2
LOG2_SCALE = math.log2(math.e) / math.sqrt(HD)


def rotary_tables(length, offset):
    half = HD // 2
    frequency = np.exp(np.arange(half) * (-2.0 * math.log(1000000.0) / HD))
    angles = (np.arange(length) + offset)[:, None] * frequency[None, :]
    cosine, sine = np.cos(angles), np.sin(angles)
    return (
        jnp.asarray(np.concatenate([cosine, cosine], axis=1), jnp.float32),
        jnp.asarray(np.concatenate([-sine, sine], axis=1), jnp.float32),
    )


def rotate(values, cosine, signed_sine):
    floats = values.astype(jnp.float32)
    swapped = pltpu.roll(floats, HD // 2, 1)
    return (floats * cosine + swapped * signed_sine).astype(jnp.bfloat16)


def dot_keys(queries, keys):
    return lax.dot_general(
        queries, keys, (((1,), (1,)), ((), ())), preferred_element_type=jnp.float32
    )


def dot_values(weights, values):
    extended = jnp.concatenate([values, jnp.ones_like(values)], axis=1)
    return jnp.dot(weights, extended, preferred_element_type=jnp.float32)


def exchange_and_attend(
    n, q_hbm, seg_hbm, prefix_hbm, pool_hbm, slots_ref, cos_ref, sin_ref, version_ref, count_ref,
    out_hbm,
    q_ref, seg_ref, prefix_ref, pool_ref, asked_ref, asked_smem, stage_ref, page_ref,
    rot_ref, acc_ref, max_ref, sum_ref, key_ref, value_ref,
    load_sem, ask_send, ask_recv, ask_sem, page_send, page_recv, out_sem,
):
    myself = lax.axis_index("prob")
    beams, seg_len, model_width = q_ref.shape
    kv_heads = rot_ref.shape[1]
    group = model_width // HD // kv_heads
    rows = group * seg_len
    rounds, capacity = stage_ref.shape[:2]
    pages = version_ref.shape[2]
    page_len = pool_ref.shape[1] // 2
    remote = [r for r in range(rounds) if (r + 1) % n]

    loads = [
        pltpu.make_async_copy(source, target, load_sem.at[i])
        for i, (source, target) in enumerate(
            (
                (pool_hbm, pool_ref),
                (prefix_hbm.at[0], prefix_ref),
                (seg_hbm.at[0], seg_ref),
                (q_hbm.at[0], q_ref),
            )
        )
    ]
    for load in loads:
        load.start()

    shifts = sorted({(1 + r) % n for r in remote} | {(-1 - r) % n for r in remote})
    barrier = pltpu.get_barrier_semaphore()
    for shift in shifts:
        pl.semaphore_signal(
            barrier, inc=1, device_id={"prob": lax.rem(myself + shift, n)}, device_id_type=MESH
        )
    pl.semaphore_wait(barrier, len(shifts))

    def ask(r):
        return pltpu.make_async_remote_copy(
            src_ref=slots_ref.at[r],
            dst_ref=asked_ref.at[r],
            send_sem=ask_send.at[r],
            recv_sem=ask_recv.at[r],
            device_id={"prob": lax.rem(myself + (1 + r) % n, n)},
            device_id_type=MESH,
        )

    def serve(r):
        return pltpu.make_async_remote_copy(
            src_ref=stage_ref.at[r],
            dst_ref=page_ref.at[r],
            send_sem=page_send.at[r],
            recv_sem=page_recv.at[r],
            device_id={"prob": lax.rem(myself + (-1 - r) % n, n)},
            device_id_type=MESH,
        )

    for r in remote:
        ask(r).start()
    for r in range(rounds):
        if r not in remote:
            asked_ref[r] = slots_ref[r]
    loads[0].wait()
    for r in remote:
        ask(r).wait_recv()
    table = pltpu.make_async_copy(asked_ref, asked_smem, ask_sem)
    table.start()
    table.wait()
    for r in sorted(range(rounds), key=lambda r: -min((r + 1) % n, (-1 - r) % n)):
        for c in range(capacity):
            page = pool_ref[asked_smem[r, 0, c]]
            if r in remote:
                stage_ref[r, c] = page
            else:
                page_ref[r, c] = page
        if r in remote:
            serve(r).start()
    for load in loads[1:]:
        load.wait()

    cosine, sine = cos_ref[...], sin_ref[...]
    token = lax.broadcasted_iota(jnp.int32, (group, seg_len, seg_len), 1).reshape(rows, seg_len)
    causal = token >= lax.broadcasted_iota(jnp.int32, (rows, seg_len), 1)

    def column(number):
        return pl.ds(pl.multiple_of(number * HD, HD), HD)

    def local_step(step, carry):
        beam, head = step // kv_heads, step % kv_heads
        queries = jnp.concatenate(
            [
                rotate(q_ref[beam, :, column(head * group + g)], cosine, sine)
                for g in range(group)
            ],
            axis=0,
        )
        fresh_keys = rotate(seg_ref[beam, 0, :, column(head)], cosine, sine)
        prefix_scores = dot_keys(queries, prefix_ref[0, :, column(head)])
        fresh_scores = jnp.where(causal, dot_keys(queries, fresh_keys), NEG_FILL)
        row_max = jnp.maximum(
            prefix_scores.max(-1, keepdims=True), fresh_scores.max(-1, keepdims=True)
        )
        shift = row_max * LOG2_SCALE
        prefix_exp = jnp.exp2(prefix_scores * LOG2_SCALE - shift).astype(jnp.bfloat16)
        fresh_exp = jnp.exp2(fresh_scores * LOG2_SCALE - shift).astype(jnp.bfloat16)
        mixed = dot_values(prefix_exp, prefix_ref[1, :, column(head)]) + dot_values(
            fresh_exp, seg_ref[beam, 1, :, column(head)]
        )
        rot_ref[beam, head] = queries
        acc_ref[beam, head] = mixed[:, :HD]
        sum_ref[beam, head] = mixed[:, HD:]
        max_ref[beam, head] = jnp.broadcast_to(shift, (rows, HD))
        return carry

    lax.fori_loop(0, beams * kv_heads, local_step, 0)

    for r in remote:
        serve(r).wait_recv()

    def store(beam):
        return pltpu.make_async_copy(q_ref.at[beam], out_hbm.at[0, beam], out_sem.at[beam])

    def beam_step(beam, carry):
        live = beam < count_ref[0]

        def fetched(j):
            number = j * beams + version_ref[0, beam, j]
            page = page_ref[lax.rem(number, n), lax.div(number, n)].astype(jnp.float32)
            return page[:page_len], page[page_len:]

        for j in range(0, pages, 2):
            first, second = fetched(j), fetched(j + 1)
            span = pl.ds(j * page_len, 2 * page_len)
            key_ref[span] = jnp.concatenate([first[0], second[0]], axis=0).astype(jnp.bfloat16)
            value_ref[span] = jnp.concatenate([first[1], second[1]], axis=0).astype(jnp.bfloat16)

        def head_step(head):
            scores = dot_keys(rot_ref[beam, head], key_ref[:, column(head)]) * LOG2_SCALE
            old_shift = max_ref[beam, head]
            shift = jnp.maximum(old_shift, scores.max(-1, keepdims=True))
            weights = jnp.exp2(scores - shift[:, :1]).astype(jnp.bfloat16)
            decay = jnp.exp2(old_shift - shift)
            mixed = dot_values(weights, value_ref[:, column(head)])
            total = mixed[:, HD:] + sum_ref[beam, head] * decay
            result = (mixed[:, :HD] + acc_ref[beam, head] * decay) / total
            result = jnp.where(live, result, 0.0).astype(jnp.bfloat16)
            for g in range(group):
                q_ref[beam, :, column(head * group + g)] = result[g * seg_len : (g + 1) * seg_len]

        def heads_step(step, inner):
            for k in range(UNROLL):
                head_step(step * UNROLL + k)
            return inner

        lax.fori_loop(0, kv_heads // UNROLL, heads_step, 0)
        store(beam).start()
        return carry

    lax.fori_loop(0, beams, beam_step, 0)
    for beam in range(beams):
        store(beam).wait()
    for r in remote:
        ask(r).wait_send()
        serve(r).wait_send()


def per_device(
    segment_queries, segment_kv, prefix_kv, page_pool, beam_count, page_version, page_slot
):
    devices = lax.axis_size("prob")
    _, beams, seg_len, model_width = segment_queries.shape
    shared = prefix_kv.shape[2]
    pool_pages, _, page_len, kv_width = page_pool.shape
    context_pages = page_version.shape[2]
    kv_heads = kv_width // HD
    rows = model_width // kv_width * seg_len
    rounds = min(devices, pool_pages)
    capacity = (pool_pages + devices - 1) // devices
    cosine, sine = rotary_tables(seg_len, shared + context_pages * page_len)
    slots = page_slot.reshape(-1)
    slots = jnp.pad(slots, (0, capacity * rounds - slots.shape[0]))
    slots = slots.reshape(capacity, rounds).T[:, None, :]
    slots = jnp.pad(slots, ((0, 0), (0, 0), (0, HD - capacity)))

    any_spec = pl.BlockSpec(memory_space=pl.ANY)
    vmem_spec = pl.BlockSpec(memory_space=pltpu.VMEM)
    smem_spec = pl.BlockSpec(memory_space=pltpu.SMEM)
    page_block = (rounds, capacity, 2 * page_len, kv_width)
    state = (beams, kv_heads, rows, HD)
    dma = pltpu.SemaphoreType.DMA
    positions = shared + seg_len + context_pages * page_len
    return pl.pallas_call(
        functools.partial(exchange_and_attend, devices),
        in_specs=[any_spec] * 4 + [vmem_spec] * 3 + [smem_spec] * 2,
        out_specs=any_spec,
        out_shape=jax.ShapeDtypeStruct(segment_queries.shape, jnp.bfloat16),
        scratch_shapes=[
            pltpu.VMEM(segment_queries.shape[1:], jnp.bfloat16),
            pltpu.VMEM(segment_kv.shape[1:], jnp.bfloat16),
            pltpu.VMEM(prefix_kv.shape[1:], jnp.bfloat16),
            pltpu.VMEM((pool_pages, 2 * page_len, kv_width), jnp.bfloat16),
            pltpu.VMEM((rounds, 1, HD), jnp.int32),
            pltpu.SMEM((rounds, 1, HD), jnp.int32),
            pltpu.VMEM(page_block, jnp.bfloat16),
            pltpu.VMEM(page_block, jnp.bfloat16),
            pltpu.VMEM(state, jnp.bfloat16),
            pltpu.VMEM(state, jnp.float32),
            pltpu.VMEM(state, jnp.float32),
            pltpu.VMEM(state, jnp.float32),
            pltpu.VMEM((context_pages * page_len, kv_width), jnp.bfloat16),
            pltpu.VMEM((context_pages * page_len, kv_width), jnp.bfloat16),
            dma((4,)),
            dma((rounds,)),
            dma((rounds,)),
            dma(()),
            dma((rounds,)),
            dma((rounds,)),
            dma((beams,)),
        ],
        compiler_params=pltpu.CompilerParams(
            collective_id=0, has_side_effects=True, vmem_limit_bytes=56 * 1024 * 1024
        ),
        cost_estimate=pl.CostEstimate(
            flops=4 * beams * kv_heads * rows * HD * positions,
            bytes_accessed=14 * 1024 * 1024,
            transcendentals=beams * kv_heads * rows * positions,
        ),
        name="exchange_and_attend",
    )(
        segment_queries,
        segment_kv,
        prefix_kv,
        page_pool.reshape(pool_pages, 2 * page_len, kv_width),
        slots,
        cosine,
        sine,
        page_version,
        beam_count,
    )


def solution(mesh):
    placed = (
        P(("groups", "prob"), None, None, None),
        P(("groups", "prob"), None, None, None, None),
        P(("groups", "prob"), None, None, None),
        P(("groups", "prob"), None, None, None),
        P(("groups", "prob")),
        P(("groups", "prob"), None, None),
        P(("groups", "prob"), None, None),
    )
    return jax.shard_map(
        per_device,
        mesh=mesh,
        in_specs=placed,
        out_specs=P(("groups", "prob"), None, None, None),
        check_vma=False,
    )
```

```python
import functools
import math

import jax
import jax.numpy as jnp
import numpy as np
from jax import lax
from jax.experimental import pallas as pl
from jax.experimental.pallas import tpu as pltpu
from jax.sharding import PartitionSpec as P

HD = 128
NEG_FILL = -1e30
MESH = pl.DeviceIdType.MESH
UNROLL = 2
LOG2_SCALE = math.log2(math.e) / math.sqrt(HD)


def rotary_tables(length, offset):
    half = HD // 2
    frequency = np.exp(np.arange(half) * (-2.0 * math.log(1000000.0) / HD))
    angles = (np.arange(length) + offset)[:, None] * frequency[None, :]
    cosine, sine = np.cos(angles), np.sin(angles)
    return (
        jnp.asarray(np.concatenate([cosine, cosine], axis=1), jnp.float32),
        jnp.asarray(np.concatenate([-sine, sine], axis=1), jnp.float32),
    )


def rotate(values, cosine, signed_sine):
    floats = values.astype(jnp.float32)
    swapped = pltpu.roll(floats, HD // 2, 1)
    return (floats * cosine + swapped * signed_sine).astype(jnp.bfloat16)


def dot_keys(queries, keys):
    return lax.dot_general(
        queries, keys, (((1,), (1,)), ((), ())), preferred_element_type=jnp.float32
    )


def dot_values(weights, values):
    extended = jnp.concatenate([values, jnp.ones_like(values)], axis=1)
    return jnp.dot(weights, extended, preferred_element_type=jnp.float32)


def exchange_and_attend(
    n, q_hbm, seg_hbm, prefix_hbm, pool_hbm, slots_ref, cos_ref, sin_ref, version_ref, count_ref,
    out_hbm,
    q_ref, seg_ref, prefix_ref, pool_ref, asked_ref, asked_smem, stage_ref, page_ref,
    rot_ref, acc_ref, max_ref, sum_ref, key_ref, value_ref,
    load_sem, ask_send, ask_recv, ask_sem, page_send, page_recv, out_sem,
):
    myself = lax.axis_index("prob")
    beams, seg_len, model_width = q_ref.shape
    kv_heads = rot_ref.shape[1]
    group = model_width // HD // kv_heads
    rows = group * seg_len
    rounds, capacity = stage_ref.shape[:2]
    pages = version_ref.shape[2]
    copies = slots_ref.shape[1]
    page_len = pool_ref.shape[1] // 2
    remote = [r for r in range(rounds) if (r + 1) % n]

    loads = [
        pltpu.make_async_copy(source, target, load_sem.at[i])
        for i, (source, target) in enumerate(
            (
                (pool_hbm, pool_ref),
                (prefix_hbm.at[0], prefix_ref),
                (seg_hbm.at[0], seg_ref),
                (q_hbm.at[0], q_ref),
            )
        )
    ]
    for load in loads:
        load.start()

    shifts = sorted({(1 + r) % n for r in remote} | {(-1 - r) % n for r in remote})
    barrier = pltpu.get_barrier_semaphore()
    for shift in shifts:
        pl.semaphore_signal(
            barrier, inc=1, device_id={"prob": lax.rem(myself + shift, n)}, device_id_type=MESH
        )
    pl.semaphore_wait(barrier, len(shifts))

    def ask(r):
        return pltpu.make_async_remote_copy(
            src_ref=slots_ref,
            dst_ref=asked_ref.at[r],
            send_sem=ask_send.at[r],
            recv_sem=ask_recv.at[r],
            device_id={"prob": lax.rem(myself + (1 + r) % n, n)},
            device_id_type=MESH,
        )

    def serve(r):
        return pltpu.make_async_remote_copy(
            src_ref=stage_ref.at[r],
            dst_ref=page_ref.at[r],
            send_sem=page_send.at[r],
            recv_sem=page_recv.at[r],
            device_id={"prob": lax.rem(myself + (-1 - r) % n, n)},
            device_id_type=MESH,
        )

    for r in remote:
        ask(r).start()
    for r in range(rounds):
        if r not in remote:
            asked_ref[r] = slots_ref[...]
    loads[0].wait()
    for r in remote:
        ask(r).wait_recv()
    table = pltpu.make_async_copy(asked_ref, asked_smem, ask_sem)
    table.start()
    table.wait()
    for r in sorted(range(rounds), key=lambda r: (r % beams, -min((r + 1) % n, (-1 - r) % n))):
        for c in range(capacity):
            page = pool_ref[asked_smem[r, 0, min(r + c * n, copies - 1)]]
            if r in remote:
                stage_ref[r, c] = page
            else:
                page_ref[r, c] = page
        if r in remote:
            serve(r).start()
    for load in loads[1:]:
        load.wait()

    cosine, sine = cos_ref[...], sin_ref[...]
    token = lax.broadcasted_iota(jnp.int32, (group, seg_len, seg_len), 1).reshape(rows, seg_len)
    causal = token >= lax.broadcasted_iota(jnp.int32, (rows, seg_len), 1)

    def column(number):
        return pl.ds(pl.multiple_of(number * HD, HD), HD)

    def local_step(step, carry):
        beam, head = step // kv_heads, step % kv_heads
        queries = jnp.concatenate(
            [
                rotate(q_ref[beam, :, column(head * group + g)], cosine, sine)
                for g in range(group)
            ],
            axis=0,
        )
        fresh_keys = rotate(seg_ref[beam, 0, :, column(head)], cosine, sine)
        prefix_scores = dot_keys(queries, prefix_ref[0, :, column(head)])
        fresh_scores = jnp.where(causal, dot_keys(queries, fresh_keys), NEG_FILL)
        row_max = jnp.maximum(
            prefix_scores.max(-1, keepdims=True), fresh_scores.max(-1, keepdims=True)
        )
        shift = row_max * LOG2_SCALE
        prefix_exp = jnp.exp2(prefix_scores * LOG2_SCALE - shift).astype(jnp.bfloat16)
        fresh_exp = jnp.exp2(fresh_scores * LOG2_SCALE - shift).astype(jnp.bfloat16)
        mixed = dot_values(prefix_exp, prefix_ref[1, :, column(head)]) + dot_values(
            fresh_exp, seg_ref[beam, 1, :, column(head)]
        )
        rot_ref[beam, head] = queries
        acc_ref[beam, head] = mixed[:, :HD]
        sum_ref[beam, head] = mixed[:, HD:]
        max_ref[beam, head] = jnp.broadcast_to(shift, (rows, HD))
        return carry

    lax.fori_loop(0, beams * kv_heads, local_step, 0)

    def store(beam):
        return pltpu.make_async_copy(q_ref.at[beam], out_hbm.at[0, beam], out_sem.at[beam])

    def beam_step(beam):
        live = beam < count_ref[0]
        for r in remote:
            if r % beams == beam:
                serve(r).wait_recv()

        def fetched(j):
            version = version_ref[0, beam, j]
            page = None
            for candidate in range(beam + 1):
                number = j * beams + candidate
                stored = page_ref[number % n, number // n]
                page = stored if page is None else jnp.where(version == candidate, stored, page)
            page = page.astype(jnp.float32)
            return page[:page_len], page[page_len:]

        for j in range(0, pages, 2):
            first, second = fetched(j), fetched(j + 1)
            span = pl.ds(j * page_len, 2 * page_len)
            key_ref[span] = jnp.concatenate([first[0], second[0]], axis=0).astype(jnp.bfloat16)
            value_ref[span] = jnp.concatenate([first[1], second[1]], axis=0).astype(jnp.bfloat16)

        def head_step(head):
            scores = dot_keys(rot_ref[beam, head], key_ref[:, column(head)]) * LOG2_SCALE
            old_shift = max_ref[beam, head]
            shift = jnp.maximum(old_shift, scores.max(-1, keepdims=True))
            weights = jnp.exp2(scores - shift[:, :1]).astype(jnp.bfloat16)
            decay = jnp.exp2(old_shift - shift)
            mixed = dot_values(weights, value_ref[:, column(head)])
            total = mixed[:, HD:] + sum_ref[beam, head] * decay
            result = (mixed[:, :HD] + acc_ref[beam, head] * decay) / total
            result = jnp.where(live, result, 0.0).astype(jnp.bfloat16)
            for g in range(group):
                q_ref[beam, :, column(head * group + g)] = result[g * seg_len : (g + 1) * seg_len]

        def heads_step(step, inner):
            for k in range(UNROLL):
                head_step(step * UNROLL + k)
            return inner

        lax.fori_loop(0, kv_heads // UNROLL, heads_step, 0)
        store(beam).start()

    for beam in range(beams):
        beam_step(beam)
    for beam in range(beams):
        store(beam).wait()
    for r in remote:
        ask(r).wait_send()
        serve(r).wait_send()


def per_device(
    segment_queries, segment_kv, prefix_kv, page_pool, beam_count, page_version, page_slot
):
    devices = lax.axis_size("prob")
    _, beams, seg_len, model_width = segment_queries.shape
    shared = prefix_kv.shape[2]
    pool_pages, _, page_len, kv_width = page_pool.shape
    context_pages = page_version.shape[2]
    kv_heads = kv_width // HD
    rows = model_width // kv_width * seg_len
    rounds = min(devices, pool_pages)
    capacity = (pool_pages + devices - 1) // devices
    cosine, sine = rotary_tables(seg_len, shared + context_pages * page_len)
    slots = page_slot.reshape(1, pool_pages)

    any_spec = pl.BlockSpec(memory_space=pl.ANY)
    vmem_spec = pl.BlockSpec(memory_space=pltpu.VMEM)
    smem_spec = pl.BlockSpec(memory_space=pltpu.SMEM)
    page_block = (rounds, capacity, 2 * page_len, kv_width)
    state = (beams, kv_heads, rows, HD)
    dma = pltpu.SemaphoreType.DMA
    positions = shared + seg_len + context_pages * page_len
    return pl.pallas_call(
        functools.partial(exchange_and_attend, devices),
        in_specs=[any_spec] * 4 + [vmem_spec] * 3 + [smem_spec] * 2,
        out_specs=any_spec,
        out_shape=jax.ShapeDtypeStruct(segment_queries.shape, jnp.bfloat16),
        scratch_shapes=[
            pltpu.VMEM(segment_queries.shape[1:], jnp.bfloat16),
            pltpu.VMEM(segment_kv.shape[1:], jnp.bfloat16),
            pltpu.VMEM(prefix_kv.shape[1:], jnp.bfloat16),
            pltpu.VMEM((pool_pages, 2 * page_len, kv_width), jnp.bfloat16),
            pltpu.VMEM((rounds, 1, pool_pages), jnp.int32),
            pltpu.SMEM((rounds, 1, pool_pages), jnp.int32),
            pltpu.VMEM(page_block, jnp.bfloat16),
            pltpu.VMEM(page_block, jnp.bfloat16),
            pltpu.VMEM(state, jnp.bfloat16),
            pltpu.VMEM(state, jnp.float32),
            pltpu.VMEM(state, jnp.float32),
            pltpu.VMEM(state, jnp.float32),
            pltpu.VMEM((context_pages * page_len, kv_width), jnp.bfloat16),
            pltpu.VMEM((context_pages * page_len, kv_width), jnp.bfloat16),
            dma((4,)),
            dma((rounds,)),
            dma((rounds,)),
            dma(()),
            dma((rounds,)),
            dma((rounds,)),
            dma((beams,)),
        ],
        compiler_params=pltpu.CompilerParams(
            collective_id=0, has_side_effects=True, vmem_limit_bytes=56 * 1024 * 1024
        ),
        cost_estimate=pl.CostEstimate(
            flops=4 * beams * kv_heads * rows * HD * positions,
            bytes_accessed=14 * 1024 * 1024,
            transcendentals=beams * kv_heads * rows * positions,
        ),
        name="exchange_and_attend",
    )(
        segment_queries,
        segment_kv,
        prefix_kv,
        page_pool.reshape(pool_pages, 2 * page_len, kv_width),
        slots,
        cosine,
        sine,
        page_version,
        beam_count,
    )


def solution(mesh):
    placed = (
        P(("groups", "prob"), None, None, None),
        P(("groups", "prob"), None, None, None, None),
        P(("groups", "prob"), None, None, None),
        P(("groups", "prob"), None, None, None),
        P(("groups", "prob")),
        P(("groups", "prob"), None, None),
        P(("groups", "prob"), None, None),
    )
    return jax.shard_map(
        per_device,
        mesh=mesh,
        in_specs=placed,
        out_specs=P(("groups", "prob"), None, None, None),
        check_vma=False,
    )
```

```python
import functools
import math

import jax
import jax.numpy as jnp
import numpy as np
from jax import lax
from jax.experimental import pallas as pl
from jax.experimental.pallas import tpu as pltpu
from jax.sharding import PartitionSpec as P

HD = 128
NEG_FILL = -1e30
MESH = pl.DeviceIdType.MESH
UNROLL = 2
LOG2_SCALE = math.log2(math.e) / math.sqrt(HD)


def rotary_tables(length, offset):
    half = HD // 2
    frequency = np.exp(np.arange(half) * (-2.0 * math.log(1000000.0) / HD))
    angles = (np.arange(length) + offset)[:, None] * frequency[None, :]
    cosine, sine = np.cos(angles), np.sin(angles)
    return (
        jnp.asarray(np.concatenate([cosine, cosine], axis=1), jnp.float32),
        jnp.asarray(np.concatenate([-sine, sine], axis=1), jnp.float32),
    )


def rotate(values, cosine, signed_sine):
    floats = values.astype(jnp.float32)
    swapped = pltpu.roll(floats, HD // 2, 1)
    return (floats * cosine + swapped * signed_sine).astype(jnp.bfloat16)


def dot_keys(queries, keys):
    return lax.dot_general(
        queries, keys, (((1,), (1,)), ((), ())), preferred_element_type=jnp.float32
    )


def dot_values(weights, values):
    extended = jnp.concatenate([values, jnp.ones_like(values)], axis=1)
    return jnp.dot(weights, extended, preferred_element_type=jnp.float32)


def exchange_and_attend(
    n, q_hbm, seg_hbm, prefix_hbm, pool_hbm, slots_ref, cos_ref, sin_ref, version_ref, count_ref,
    out_hbm, rot_hbm, acc_hbm, max_hbm, sum_hbm, key_hbm, value_hbm,
    q_ref, seg_ref, prefix_ref, pool_ref, asked_ref, asked_smem, stage_ref, page_ref,
    rot_ref, acc_ref, max_ref, sum_ref, key_ref, value_ref,
    load_sem, ask_send, ask_recv, ask_sem, page_send, page_recv, out_sem, state_sem,
):
    myself = lax.axis_index("prob")
    beams, seg_len, model_width = q_ref.shape
    kv_heads = rot_ref.shape[1]
    group = model_width // HD // kv_heads
    rows = group * seg_len
    rounds, capacity = stage_ref.shape[:2]
    pages = version_ref.shape[2]
    copies = slots_ref.shape[1]
    page_len = pool_ref.shape[1] // 2
    remote = [r for r in range(rounds) if (r + 1) % n]

    loads = [
        pltpu.make_async_copy(source, target, load_sem.at[i])
        for i, (source, target) in enumerate(
            (
                (pool_hbm, pool_ref),
                (prefix_hbm.at[0], prefix_ref),
                (seg_hbm.at[0], seg_ref),
                (q_hbm.at[0], q_ref),
            )
        )
    ]
    for load in loads:
        load.start()

    shifts = sorted({(1 + r) % n for r in remote} | {(-1 - r) % n for r in remote})
    barrier = pltpu.get_barrier_semaphore()
    for shift in shifts:
        pl.semaphore_signal(
            barrier, inc=1, device_id={"prob": lax.rem(myself + shift, n)}, device_id_type=MESH
        )
    pl.semaphore_wait(barrier, len(shifts))

    def ask(r):
        return pltpu.make_async_remote_copy(
            src_ref=slots_ref,
            dst_ref=asked_ref.at[r],
            send_sem=ask_send.at[r],
            recv_sem=ask_recv.at[r],
            device_id={"prob": lax.rem(myself + (1 + r) % n, n)},
            device_id_type=MESH,
        )

    def serve(r):
        return pltpu.make_async_remote_copy(
            src_ref=stage_ref.at[r],
            dst_ref=page_ref.at[r],
            send_sem=page_send.at[r],
            recv_sem=page_recv.at[r],
            device_id={"prob": lax.rem(myself + (-1 - r) % n, n)},
            device_id_type=MESH,
        )

    for r in remote:
        ask(r).start()
    for r in range(rounds):
        if r not in remote:
            asked_ref[r] = slots_ref[...]
    loads[0].wait()
    for r in remote:
        ask(r).wait_recv()
    table = pltpu.make_async_copy(asked_ref, asked_smem, ask_sem)
    table.start()
    table.wait()
    for r in sorted(range(rounds), key=lambda r: (r % beams, -min((r + 1) % n, (-1 - r) % n))):
        for c in range(capacity):
            page = pool_ref[asked_smem[r, 0, min(r + c * n, copies - 1)]]
            if r in remote:
                stage_ref[r, c] = page
            else:
                page_ref[r, c] = page
        if r in remote:
            serve(r).start()
    for load in loads[1:]:
        load.wait()

    cosine, sine = cos_ref[...], sin_ref[...]
    token = lax.broadcasted_iota(jnp.int32, (group, seg_len, seg_len), 1).reshape(rows, seg_len)
    causal = token >= lax.broadcasted_iota(jnp.int32, (rows, seg_len), 1)

    def column(number):
        return pl.ds(pl.multiple_of(number * HD, HD), HD)

    def local_step(step, carry):
        beam, head = step // kv_heads, step % kv_heads
        queries = jnp.concatenate(
            [
                rotate(q_ref[beam, :, column(head * group + g)], cosine, sine)
                for g in range(group)
            ],
            axis=0,
        )
        fresh_keys = rotate(seg_ref[beam, 0, :, column(head)], cosine, sine)
        prefix_scores = dot_keys(queries, prefix_ref[0, :, column(head)])
        fresh_scores = jnp.where(causal, dot_keys(queries, fresh_keys), NEG_FILL)
        row_max = jnp.maximum(
            prefix_scores.max(-1, keepdims=True), fresh_scores.max(-1, keepdims=True)
        )
        shift = row_max * LOG2_SCALE
        prefix_exp = jnp.exp2(prefix_scores * LOG2_SCALE - shift).astype(jnp.bfloat16)
        fresh_exp = jnp.exp2(fresh_scores * LOG2_SCALE - shift).astype(jnp.bfloat16)
        mixed = dot_values(prefix_exp, prefix_ref[1, :, column(head)]) + dot_values(
            fresh_exp, seg_ref[beam, 1, :, column(head)]
        )
        rot_ref[beam, head] = queries
        acc_ref[beam, head] = mixed[:, :HD]
        sum_ref[beam, head] = mixed[:, HD:]
        max_ref[beam, head] = jnp.broadcast_to(shift, (rows, HD))
        return carry

    lax.fori_loop(0, beams * kv_heads, local_step, 0)
    last = beams - 1
    state = [
        pltpu.make_async_copy(source, target, state_sem.at[i])
        for i, (source, target) in enumerate(
            (
                (rot_ref.at[last], rot_hbm),
                (acc_ref.at[last], acc_hbm),
                (max_ref.at[last], max_hbm),
                (sum_ref.at[last], sum_hbm),
                (key_ref, key_hbm),
                (value_ref, value_hbm),
            )
        )
    ]
    for copy in state[:4]:
        copy.start()

    def store(beam):
        return pltpu.make_async_copy(q_ref.at[beam], out_hbm.at[0, beam], out_sem.at[beam])

    def beam_step(beam):
        live = beam < count_ref[0]
        for r in remote:
            if r % beams == beam:
                serve(r).wait_recv()

        def fetched(j):
            version = version_ref[0, beam, j]
            page = None
            for candidate in range(beam + 1):
                number = j * beams + candidate
                stored = page_ref[number % n, number // n]
                page = stored if page is None else jnp.where(version == candidate, stored, page)
            page = page.astype(jnp.float32)
            return page[:page_len], page[page_len:]

        for j in range(0, pages, 2):
            first, second = fetched(j), fetched(j + 1)
            span = pl.ds(j * page_len, 2 * page_len)
            key_ref[span] = jnp.concatenate([first[0], second[0]], axis=0).astype(jnp.bfloat16)
            value_ref[span] = jnp.concatenate([first[1], second[1]], axis=0).astype(jnp.bfloat16)

        if beam == last:
            for copy in state[4:]:
                copy.start()
            return

        def head_step(head):
            scores = dot_keys(rot_ref[beam, head], key_ref[:, column(head)]) * LOG2_SCALE
            old_shift = max_ref[beam, head]
            shift = jnp.maximum(old_shift, scores.max(-1, keepdims=True))
            weights = jnp.exp2(scores - shift[:, :1]).astype(jnp.bfloat16)
            decay = jnp.exp2(old_shift - shift)
            mixed = dot_values(weights, value_ref[:, column(head)])
            total = mixed[:, HD:] + sum_ref[beam, head] * decay
            result = (mixed[:, :HD] + acc_ref[beam, head] * decay) / total
            result = jnp.where(live, result, 0.0).astype(jnp.bfloat16)
            for g in range(group):
                q_ref[beam, :, column(head * group + g)] = result[g * seg_len : (g + 1) * seg_len]

        def heads_step(step, inner):
            for k in range(UNROLL):
                head_step(step * UNROLL + k)
            return inner

        lax.fori_loop(0, kv_heads // UNROLL, heads_step, 0)
        store(beam).start()

    for beam in range(beams):
        beam_step(beam)
    for beam in range(last):
        store(beam).wait()
    for copy in state:
        copy.wait()
    for r in remote:
        ask(r).wait_send()
        serve(r).wait_send()


def last_beam(
    count_ref, done_hbm, rot_ref, acc_ref, max_ref, sum_ref, key_ref, value_ref,
    out_hbm, out_ref, done_sem, out_sem,
):
    step = pl.program_id(0)
    steps = pl.num_programs(0)
    done = done_hbm.shape[1]
    seg_len = out_ref.shape[1]
    heads, rows = rot_ref.shape[:2]
    group = rows // seg_len
    width = out_ref.shape[2]
    live = done < count_ref[0]

    def forward(beam):
        return pltpu.make_async_copy(done_hbm.at[0, beam], out_hbm.at[0, beam], done_sem.at[beam])

    def store(number):
        start = number * width
        if not isinstance(number, int):
            start = pl.multiple_of(start, HD)
        return pltpu.make_async_copy(
            out_ref.at[number], out_hbm.at[0, done, :, pl.ds(start, width)], out_sem.at[number]
        )

    @pl.when(step == 0)
    def _():
        for beam in range(done):
            forward(beam).start()

    for head in range(heads):
        columns = slice(head * HD, (head + 1) * HD)
        scores = dot_keys(rot_ref[head], key_ref[:, columns]) * LOG2_SCALE
        old_shift = max_ref[head]
        shift = jnp.maximum(old_shift, scores.max(-1, keepdims=True))
        weights = jnp.exp2(scores - shift[:, :1]).astype(jnp.bfloat16)
        decay = jnp.exp2(old_shift - shift)
        mixed = dot_values(weights, value_ref[:, columns])
        total = mixed[:, HD:] + sum_ref[head] * decay
        result = (mixed[:, :HD] + acc_ref[head] * decay) / total
        result = jnp.where(live, result, 0.0).astype(jnp.bfloat16)
        for g in range(group):
            place = (head * group + g) * HD
            out_ref[step, :, place : place + HD] = result[g * seg_len : (g + 1) * seg_len]
    store(step).start()

    @pl.when(step == steps - 1)
    def _():
        for beam in range(done):
            forward(beam).wait()
        for number in range(out_ref.shape[0]):
            store(number).wait()


def per_device(
    segment_queries, segment_kv, prefix_kv, page_pool, beam_count, page_version, page_slot
):
    devices = lax.axis_size("prob")
    _, beams, seg_len, model_width = segment_queries.shape
    shared = prefix_kv.shape[2]
    pool_pages, _, page_len, kv_width = page_pool.shape
    context_pages = page_version.shape[2]
    kv_heads = kv_width // HD
    rows = model_width // kv_width * seg_len
    rounds = min(devices, pool_pages)
    capacity = (pool_pages + devices - 1) // devices
    cosine, sine = rotary_tables(seg_len, shared + context_pages * page_len)
    slots = page_slot.reshape(1, pool_pages)

    any_spec = pl.BlockSpec(memory_space=pl.ANY)
    vmem_spec = pl.BlockSpec(memory_space=pltpu.VMEM)
    smem_spec = pl.BlockSpec(memory_space=pltpu.SMEM)
    page_block = (rounds, capacity, 2 * page_len, kv_width)
    state = (beams, kv_heads, rows, HD)
    dma = pltpu.SemaphoreType.DMA
    positions = shared + seg_len + context_pages * page_len
    span = (context_pages * page_len, kv_width)
    finished, *partial = pl.pallas_call(
        functools.partial(exchange_and_attend, devices),
        in_specs=[any_spec] * 4 + [vmem_spec] * 3 + [smem_spec] * 2,
        out_specs=[any_spec] * 7,
        out_shape=[
            jax.ShapeDtypeStruct((1, beams - 1, seg_len, model_width), jnp.bfloat16),
            jax.ShapeDtypeStruct(state[1:], jnp.bfloat16),
            jax.ShapeDtypeStruct(state[1:], jnp.float32),
            jax.ShapeDtypeStruct(state[1:], jnp.float32),
            jax.ShapeDtypeStruct(state[1:], jnp.float32),
            jax.ShapeDtypeStruct(span, jnp.bfloat16),
            jax.ShapeDtypeStruct(span, jnp.bfloat16),
        ],
        scratch_shapes=[
            pltpu.VMEM(segment_queries.shape[1:], jnp.bfloat16),
            pltpu.VMEM(segment_kv.shape[1:], jnp.bfloat16),
            pltpu.VMEM(prefix_kv.shape[1:], jnp.bfloat16),
            pltpu.VMEM((pool_pages, 2 * page_len, kv_width), jnp.bfloat16),
            pltpu.VMEM((rounds, 1, pool_pages), jnp.int32),
            pltpu.SMEM((rounds, 1, pool_pages), jnp.int32),
            pltpu.VMEM(page_block, jnp.bfloat16),
            pltpu.VMEM(page_block, jnp.bfloat16),
            pltpu.VMEM(state, jnp.bfloat16),
            pltpu.VMEM(state, jnp.float32),
            pltpu.VMEM(state, jnp.float32),
            pltpu.VMEM(state, jnp.float32),
            pltpu.VMEM((context_pages * page_len, kv_width), jnp.bfloat16),
            pltpu.VMEM((context_pages * page_len, kv_width), jnp.bfloat16),
            dma((4,)),
            dma((rounds,)),
            dma((rounds,)),
            dma(()),
            dma((rounds,)),
            dma((rounds,)),
            dma((beams,)),
            dma((6,)),
        ],
        compiler_params=pltpu.CompilerParams(
            collective_id=0, has_side_effects=True, vmem_limit_bytes=56 * 1024 * 1024
        ),
        cost_estimate=pl.CostEstimate(
            flops=4 * beams * kv_heads * rows * HD * positions,
            bytes_accessed=14 * 1024 * 1024,
            transcendentals=beams * kv_heads * rows * positions,
        ),
        name="exchange_and_attend",
    )(
        segment_queries,
        segment_kv,
        prefix_kv,
        page_pool.reshape(pool_pages, 2 * page_len, kv_width),
        slots,
        cosine,
        sine,
        page_version,
        beam_count,
    )
    steps = kv_heads // UNROLL
    head_spec = pl.BlockSpec((UNROLL, rows, HD), lambda i: (i, 0, 0))
    page_spec = pl.BlockSpec((span[0], UNROLL * HD), lambda i: (0, i))
    return pl.pallas_call(
        last_beam,
        grid=(steps,),
        in_specs=[smem_spec, any_spec] + [head_spec] * 4 + [page_spec] * 2,
        out_specs=any_spec,
        out_shape=jax.ShapeDtypeStruct(segment_queries.shape, jnp.bfloat16),
        scratch_shapes=[
            pltpu.VMEM((steps, seg_len, model_width // steps), jnp.bfloat16),
            dma((beams,)),
            dma((steps,)),
        ],
        compiler_params=pltpu.CompilerParams(vmem_limit_bytes=60 * 1024 * 1024),
        name="last_beam",
    )(beam_count, finished, *partial)


def solution(mesh):
    placed = (
        P(("groups", "prob"), None, None, None),
        P(("groups", "prob"), None, None, None, None),
        P(("groups", "prob"), None, None, None),
        P(("groups", "prob"), None, None, None),
        P(("groups", "prob")),
        P(("groups", "prob"), None, None),
        P(("groups", "prob"), None, None),
    )
    return jax.shard_map(
        per_device,
        mesh=mesh,
        in_specs=placed,
        out_specs=P(("groups", "prob"), None, None, None),
        check_vma=False,
    )
```

```python
import functools
import math

import jax
import jax.numpy as jnp
import numpy as np
from jax import lax
from jax.experimental import pallas as pl
from jax.experimental.pallas import tpu as pltpu
from jax.sharding import PartitionSpec as P

HD = 128
NEG_FILL = -1e30
MESH = pl.DeviceIdType.MESH
UNROLL = 2
LOG2_SCALE = math.log2(math.e) / math.sqrt(HD)


def rotary_tables(length, offset):
    half = HD // 2
    frequency = np.exp(np.arange(half) * (-2.0 * math.log(1000000.0) / HD))
    angles = (np.arange(length) + offset)[:, None] * frequency[None, :]
    cosine, sine = np.cos(angles), np.sin(angles)
    return (
        jnp.asarray(np.concatenate([cosine, cosine], axis=1), jnp.float32),
        jnp.asarray(np.concatenate([-sine, sine], axis=1), jnp.float32),
    )


def rotate(values, cosine, signed_sine):
    floats = values.astype(jnp.float32)
    swapped = pltpu.roll(floats, HD // 2, 1)
    return (floats * cosine + swapped * signed_sine).astype(jnp.bfloat16)


def dot_keys(queries, keys):
    return lax.dot_general(
        queries, keys, (((1,), (1,)), ((), ())), preferred_element_type=jnp.float32
    )


def dot_values(weights, values):
    extended = jnp.concatenate([values, jnp.ones_like(values)], axis=1)
    return jnp.dot(weights, extended, preferred_element_type=jnp.float32)


def exchange_and_attend(
    n, q_hbm, seg_hbm, prefix_hbm, pool_hbm, slots_ref, cos_ref, sin_ref, version_ref, count_ref,
    out_hbm, rot_hbm, acc_hbm, max_hbm, sum_hbm, key_hbm, value_hbm,
    q_ref, seg_ref, prefix_ref, pool_ref, asked_ref, asked_smem, stage_ref, page_ref,
    rot_ref, acc_ref, max_ref, sum_ref, key_ref, value_ref,
    load_sem, ask_send, ask_recv, ask_sem, page_send, page_recv, out_sem, state_sem,
):
    myself = lax.axis_index("prob")
    beams, seg_len, model_width = q_ref.shape
    kv_heads = rot_ref.shape[1]
    group = model_width // HD // kv_heads
    rows = group * seg_len
    rounds, capacity = stage_ref.shape[:2]
    pages = version_ref.shape[2]
    copies = slots_ref.shape[1]
    page_len = pool_ref.shape[1] // 2
    remote = [r for r in range(rounds) if (r + 1) % n]

    loads = [
        pltpu.make_async_copy(source, target, load_sem.at[i])
        for i, (source, target) in enumerate(
            (
                (pool_hbm, pool_ref),
                (prefix_hbm.at[0], prefix_ref),
                (seg_hbm.at[0], seg_ref),
                (q_hbm.at[0], q_ref),
            )
        )
    ]
    for load in loads:
        load.start()

    shifts = sorted({(1 + r) % n for r in remote} | {(-1 - r) % n for r in remote})
    barrier = pltpu.get_barrier_semaphore()
    for shift in shifts:
        pl.semaphore_signal(
            barrier, inc=1, device_id={"prob": lax.rem(myself + shift, n)}, device_id_type=MESH
        )
    pl.semaphore_wait(barrier, len(shifts))

    def ask(r):
        return pltpu.make_async_remote_copy(
            src_ref=slots_ref,
            dst_ref=asked_ref.at[r],
            send_sem=ask_send.at[r],
            recv_sem=ask_recv.at[r],
            device_id={"prob": lax.rem(myself + (1 + r) % n, n)},
            device_id_type=MESH,
        )

    def serve(r):
        return pltpu.make_async_remote_copy(
            src_ref=stage_ref.at[r],
            dst_ref=page_ref.at[r],
            send_sem=page_send.at[r],
            recv_sem=page_recv.at[r],
            device_id={"prob": lax.rem(myself + (-1 - r) % n, n)},
            device_id_type=MESH,
        )

    for r in remote:
        ask(r).start()
    for r in range(rounds):
        if r not in remote:
            asked_ref[r] = slots_ref[...]
    loads[0].wait()
    for r in remote:
        ask(r).wait_recv()
    table = pltpu.make_async_copy(asked_ref, asked_smem, ask_sem)
    table.start()
    table.wait()
    for r in sorted(range(rounds), key=lambda r: (r % beams, -min((r + 1) % n, (-1 - r) % n))):
        for c in range(capacity):
            page = pool_ref[asked_smem[r, 0, min(r + c * n, copies - 1)]]
            if r in remote:
                stage_ref[r, c] = page
            else:
                page_ref[r, c] = page
        if r in remote:
            serve(r).start()
    for load in loads[1:]:
        load.wait()

    cosine, sine = cos_ref[...], sin_ref[...]
    token = lax.broadcasted_iota(jnp.int32, (group, seg_len, seg_len), 1).reshape(rows, seg_len)
    causal = token >= lax.broadcasted_iota(jnp.int32, (rows, seg_len), 1)

    def column(number):
        return pl.ds(pl.multiple_of(number * HD, HD), HD)

    def local_step(step, carry):
        beam, head = step // kv_heads, step % kv_heads
        queries = jnp.concatenate(
            [
                rotate(q_ref[beam, :, column(head * group + g)], cosine, sine)
                for g in range(group)
            ],
            axis=0,
        )
        fresh_keys = rotate(seg_ref[beam, 0, :, column(head)], cosine, sine)
        prefix_scores = dot_keys(queries, prefix_ref[0, :, column(head)])
        fresh_scores = jnp.where(causal, dot_keys(queries, fresh_keys), NEG_FILL)
        row_max = jnp.maximum(
            prefix_scores.max(-1, keepdims=True), fresh_scores.max(-1, keepdims=True)
        )
        shift = row_max * LOG2_SCALE
        prefix_exp = jnp.exp2(prefix_scores * LOG2_SCALE - shift).astype(jnp.bfloat16)
        fresh_exp = jnp.exp2(fresh_scores * LOG2_SCALE - shift).astype(jnp.bfloat16)
        mixed = dot_values(prefix_exp, prefix_ref[1, :, column(head)]) + dot_values(
            fresh_exp, seg_ref[beam, 1, :, column(head)]
        )
        rot_ref[beam, head] = queries
        acc_ref[beam, head] = mixed[:, :HD]
        sum_ref[beam, head] = mixed[:, HD:]
        max_ref[beam, head] = jnp.broadcast_to(shift, (rows, HD))
        return carry

    lax.fori_loop(0, beams * kv_heads, local_step, 0)
    last = beams - 1
    state = [
        pltpu.make_async_copy(source, target, state_sem.at[i])
        for i, (source, target) in enumerate(
            (
                (rot_ref.at[last], rot_hbm),
                (acc_ref.at[last], acc_hbm),
                (max_ref.at[last], max_hbm),
                (sum_ref.at[last], sum_hbm),
                (key_ref, key_hbm),
                (value_ref, value_hbm),
            )
        )
    ]
    for copy in state[:4]:
        copy.start()

    def store(beam):
        return pltpu.make_async_copy(q_ref.at[beam], out_hbm.at[0, beam], out_sem.at[beam])

    def beam_step(beam):
        live = beam < count_ref[0]
        for r in remote:
            if r % beams == beam:
                serve(r).wait_recv()

        def fetched(j):
            version = version_ref[0, beam, j]
            page = None
            for candidate in range(beam + 1):
                number = j * beams + candidate
                stored = page_ref[number % n, number // n]
                page = stored if page is None else jnp.where(version == candidate, stored, page)
            page = page.astype(jnp.float32)
            return page[:page_len], page[page_len:]

        for j in range(0, pages, 2):
            first, second = fetched(j), fetched(j + 1)
            span = pl.ds(j * page_len, 2 * page_len)
            key_ref[span] = jnp.concatenate([first[0], second[0]], axis=0).astype(jnp.bfloat16)
            value_ref[span] = jnp.concatenate([first[1], second[1]], axis=0).astype(jnp.bfloat16)

        if beam == last:
            for copy in state[4:]:
                copy.start()
            return

        def head_step(head):
            scores = dot_keys(rot_ref[beam, head], key_ref[:, column(head)]) * LOG2_SCALE
            old_shift = max_ref[beam, head]
            shift = jnp.maximum(old_shift, scores.max(-1, keepdims=True))
            weights = jnp.exp2(scores - shift[:, :1]).astype(jnp.bfloat16)
            decay = jnp.exp2(old_shift - shift)
            mixed = dot_values(weights, value_ref[:, column(head)])
            total = mixed[:, HD:] + sum_ref[beam, head] * decay
            result = (mixed[:, :HD] + acc_ref[beam, head] * decay) / total
            result = jnp.where(live, result, 0.0).astype(jnp.bfloat16)
            for g in range(group):
                q_ref[beam, :, column(head * group + g)] = result[g * seg_len : (g + 1) * seg_len]

        def heads_step(step, inner):
            for k in range(UNROLL):
                head_step(step * UNROLL + k)
            return inner

        lax.fori_loop(0, kv_heads // UNROLL, heads_step, 0)
        store(beam).start()

    for beam in range(beams):
        beam_step(beam)
    for beam in range(last):
        store(beam).wait()
    for copy in state:
        copy.wait()
    for r in remote:
        ask(r).wait_send()
        serve(r).wait_send()


def last_beam(
    count_ref, done_hbm, rot_ref, acc_ref, max_ref, sum_ref, key_ref, value_ref,
    out_hbm, out_ref, done_ref, fetch_sem, done_sem, out_sem,
):
    step = pl.program_id(0)
    steps = pl.num_programs(0)
    done = done_hbm.shape[1]
    seg_len = out_ref.shape[1]
    heads, rows = rot_ref.shape[:2]
    group = rows // seg_len
    width = out_ref.shape[2]
    live = done < count_ref[0]

    def fetch(beam):
        return pltpu.make_async_copy(done_hbm.at[0, beam], done_ref.at[beam], fetch_sem.at[beam])

    def forward(beam):
        return pltpu.make_async_copy(done_ref.at[beam], out_hbm.at[0, beam], done_sem.at[beam])

    def store(number):
        start = number * width
        if not isinstance(number, int):
            start = pl.multiple_of(start, HD)
        return pltpu.make_async_copy(
            out_ref.at[number], out_hbm.at[0, done, :, pl.ds(start, width)], out_sem.at[number]
        )

    @pl.when(step == 0)
    def _():
        for beam in range(done):
            fetch(beam).start()

    @pl.when(step == 1)
    def _():
        for beam in range(done):
            fetch(beam).wait()
            forward(beam).start()

    for head in range(heads):
        columns = slice(head * HD, (head + 1) * HD)
        scores = dot_keys(rot_ref[head], key_ref[:, columns]) * LOG2_SCALE
        old_shift = max_ref[head]
        shift = jnp.maximum(old_shift, scores.max(-1, keepdims=True))
        weights = jnp.exp2(scores - shift[:, :1]).astype(jnp.bfloat16)
        decay = jnp.exp2(old_shift - shift)
        mixed = dot_values(weights, value_ref[:, columns])
        total = mixed[:, HD:] + sum_ref[head] * decay
        result = (mixed[:, :HD] + acc_ref[head] * decay) / total
        result = jnp.where(live, result, 0.0).astype(jnp.bfloat16)
        for g in range(group):
            place = (head * group + g) * HD
            out_ref[step, :, place : place + HD] = result[g * seg_len : (g + 1) * seg_len]
    store(step).start()

    @pl.when(step == steps - 1)
    def _():
        for beam in range(done):
            forward(beam).wait()
        for number in range(out_ref.shape[0]):
            store(number).wait()


def per_device(
    segment_queries, segment_kv, prefix_kv, page_pool, beam_count, page_version, page_slot
):
    devices = lax.axis_size("prob")
    _, beams, seg_len, model_width = segment_queries.shape
    shared = prefix_kv.shape[2]
    pool_pages, _, page_len, kv_width = page_pool.shape
    context_pages = page_version.shape[2]
    kv_heads = kv_width // HD
    rows = model_width // kv_width * seg_len
    rounds = min(devices, pool_pages)
    capacity = (pool_pages + devices - 1) // devices
    cosine, sine = rotary_tables(seg_len, shared + context_pages * page_len)
    slots = page_slot.reshape(1, pool_pages)

    any_spec = pl.BlockSpec(memory_space=pl.ANY)
    vmem_spec = pl.BlockSpec(memory_space=pltpu.VMEM)
    smem_spec = pl.BlockSpec(memory_space=pltpu.SMEM)
    page_block = (rounds, capacity, 2 * page_len, kv_width)
    state = (beams, kv_heads, rows, HD)
    dma = pltpu.SemaphoreType.DMA
    positions = shared + seg_len + context_pages * page_len
    span = (context_pages * page_len, kv_width)
    finished, *partial = pl.pallas_call(
        functools.partial(exchange_and_attend, devices),
        in_specs=[any_spec] * 4 + [vmem_spec] * 3 + [smem_spec] * 2,
        out_specs=[any_spec] * 7,
        out_shape=[
            jax.ShapeDtypeStruct((1, beams - 1, seg_len, model_width), jnp.bfloat16),
            jax.ShapeDtypeStruct(state[1:], jnp.bfloat16),
            jax.ShapeDtypeStruct(state[1:], jnp.float32),
            jax.ShapeDtypeStruct(state[1:], jnp.float32),
            jax.ShapeDtypeStruct(state[1:], jnp.float32),
            jax.ShapeDtypeStruct(span, jnp.bfloat16),
            jax.ShapeDtypeStruct(span, jnp.bfloat16),
        ],
        scratch_shapes=[
            pltpu.VMEM(segment_queries.shape[1:], jnp.bfloat16),
            pltpu.VMEM(segment_kv.shape[1:], jnp.bfloat16),
            pltpu.VMEM(prefix_kv.shape[1:], jnp.bfloat16),
            pltpu.VMEM((pool_pages, 2 * page_len, kv_width), jnp.bfloat16),
            pltpu.VMEM((rounds, 1, pool_pages), jnp.int32),
            pltpu.SMEM((rounds, 1, pool_pages), jnp.int32),
            pltpu.VMEM(page_block, jnp.bfloat16),
            pltpu.VMEM(page_block, jnp.bfloat16),
            pltpu.VMEM(state, jnp.bfloat16),
            pltpu.VMEM(state, jnp.float32),
            pltpu.VMEM(state, jnp.float32),
            pltpu.VMEM(state, jnp.float32),
            pltpu.VMEM((context_pages * page_len, kv_width), jnp.bfloat16),
            pltpu.VMEM((context_pages * page_len, kv_width), jnp.bfloat16),
            dma((4,)),
            dma((rounds,)),
            dma((rounds,)),
            dma(()),
            dma((rounds,)),
            dma((rounds,)),
            dma((beams,)),
            dma((6,)),
        ],
        compiler_params=pltpu.CompilerParams(
            collective_id=0, has_side_effects=True, vmem_limit_bytes=56 * 1024 * 1024
        ),
        cost_estimate=pl.CostEstimate(
            flops=4 * beams * kv_heads * rows * HD * positions,
            bytes_accessed=14 * 1024 * 1024,
            transcendentals=beams * kv_heads * rows * positions,
        ),
        name="exchange_and_attend",
    )(
        segment_queries,
        segment_kv,
        prefix_kv,
        page_pool.reshape(pool_pages, 2 * page_len, kv_width),
        slots,
        cosine,
        sine,
        page_version,
        beam_count,
    )
    steps = kv_heads // UNROLL
    head_spec = pl.BlockSpec((UNROLL, rows, HD), lambda i: (i, 0, 0))
    page_spec = pl.BlockSpec((span[0], UNROLL * HD), lambda i: (0, i))
    return pl.pallas_call(
        last_beam,
        grid=(steps,),
        in_specs=[smem_spec, any_spec] + [head_spec] * 4 + [page_spec] * 2,
        out_specs=any_spec,
        out_shape=jax.ShapeDtypeStruct(segment_queries.shape, jnp.bfloat16),
        scratch_shapes=[
            pltpu.VMEM((steps, seg_len, model_width // steps), jnp.bfloat16),
            pltpu.VMEM((beams - 1, seg_len, model_width), jnp.bfloat16),
            dma((beams,)),
            dma((beams,)),
            dma((steps,)),
        ],
        compiler_params=pltpu.CompilerParams(vmem_limit_bytes=60 * 1024 * 1024),
        name="last_beam",
    )(beam_count, finished, *partial)


def solution(mesh):
    placed = (
        P(("groups", "prob"), None, None, None),
        P(("groups", "prob"), None, None, None, None),
        P(("groups", "prob"), None, None, None),
        P(("groups", "prob"), None, None, None),
        P(("groups", "prob")),
        P(("groups", "prob"), None, None),
        P(("groups", "prob"), None, None),
    )
    return jax.shard_map(
        per_device,
        mesh=mesh,
        in_specs=placed,
        out_specs=P(("groups", "prob"), None, None, None),
        check_vma=False,
    )
```
